32 devices in a mesh: dp: 4 (over y, x), expert: 8 (over z, core).
Axes of the slice: x: 2, y: 2, z: 4, core: 2. Of those that a mesh axis runs over, the one named last changes fastest.
Arguments:
- tokens: bfloat16 [4096, 2880], P(('dp', 'expert')), may hold values from -6 to 6
- expert_ids: int32 [4096, 4], P(('dp', 'expert')), may hold values from 0 to 7, all different within a row; in each aligned block of 128 rows (0 to 127, 128 to 255, ...) at most 128 rows name the same one
- gates: bfloat16 [4096, 4], P(('dp', 'expert')), may hold values from 0.099609375 to 1
- w_gate: bfloat16 [8, 2880, 1440], P('expert'), may hold values from -0.109375 to 0.109375
- w_up: bfloat16 [8, 2880, 1440], P('expert'), may hold values from -0.109375 to 0.109375
- w_down: bfloat16 [8, 1440, 2880], P('expert'), may hold values from -0.15625 to 0.15625
Outputs:
- mixed: bfloat16 [4096, 2880], P(('dp', 'expert'))
- expert_load: int32 [8], replicated
The draws below stay inside these ranges and needn't reach their ends.
Inputs may be any that keep to these rules, and one draw needn't show every extreme that they name: `expert_ids`: each token names 4 different experts. Among the rows of one device (aligned blocks of 128 rows) every expert is named by at most 128 rows, a bound that some block reaches.
All inputs are finite; a program needn't handle non-finite values.
Results may differ from the reference program's by a relative error of at most 0.004.
The reference program's roundings to bfloat16 on the way (of `hidden`) count: a program that leaves them out, or rounds other values in their place, can miss the bound.
Values may be sent and summed in bfloat16 or wider, within the bound.
A program may use at most 192 MiB of HBM per device.

```python
import math
import jax
import jax.numpy as jnp
import numpy as np
from jax import lax

D = 2880
FF = 1440
TOP = 4
BLOCK = 128
TOK_DEV = 128
EXPERTS = 8
TOKENS = 4096
SRC_CAP = 128
CAP = 1024
N_DP = 4


def block_scale(rng, dims, split, least, largest):
    def one(dim, shards_of):
        draws = jax.random.uniform(jax.random.fold_in(jax.random.fold_in(rng, 6), dim), (shards_of,), jnp.float32, least / len(split), largest / len(split))
        return jnp.repeat(jnp.exp(draws), dims[dim] // shards_of).reshape((-1,) + (1,) * (len(dims) - dim - 1))

    factor_of = one(*split[0])
    for cut in split[1:]:
        factor_of = factor_of * one(*cut)
    return factor_of


def shared_out(own_key, own, number, rows, amount, top, bound, lean):
    order = jax.random.permutation(own_key, amount)
    crowded, ordinary = portions_of(amount, rows * top, bound, lean, True), portions_of(amount, rows * top, bound, lean, False)
    places = jnp.arange(amount)

    def named(tallies, offset_by):
        used = int((tallies > 0).sum())
        fixed = max(1, used // 4)
        moved = fixed + (places - fixed + offset_by * (used - fixed)) % max(1, amount - fixed)
        return jnp.zeros((amount,), jnp.int32).at[order[jnp.where(places < fixed, places, moved)]].set(jnp.asarray(tallies, jnp.int32))

    tallies = jnp.where(number % 4 == 0, named(crowded, number // 4), named(ordinary, number - number // 4 - 1))
    mixed = jax.random.permutation(jax.random.fold_in(own, 3), amount)
    donor, sink = mixed[0:amount // 2 * 2:2], mixed[1:amount // 2 * 2:2]
    room = jnp.minimum(tallies[donor] - 1, bound - tallies[sink]) // 2
    room = jnp.where((donor == order[0]) | (sink == order[0]) | (tallies[sink] == 0), 0, jnp.maximum(room, 0))
    moved = jax.random.randint(jax.random.fold_in(own, 4), (amount // 2,), 0, 1 << 20) % (room + 1)
    tallies = tallies.at[donor].add(-moved).at[sink].add(moved)
    members = jnp.searchsorted(jnp.cumsum(tallies), jnp.arange(rows * top), side="right").astype(jnp.int32)
    grid = members.reshape(top, rows).T
    grid = grid[jax.random.permutation(jax.random.fold_in(own, 1), rows)]
    offset_by = jax.random.randint(jax.random.fold_in(own, 2), (rows, 1), 0, top)
    return jnp.take_along_axis(grid, (jnp.arange(top)[None, :] + offset_by) % top, axis=1)


def portions_of(number_of, total, limit, skew, full):
    portions = [(1 << 20) // math.isqrt(grade ** skew) + 1 for grade in range(1, number_of + 1)]
    largest = limit if full else min(limit, max(-(-total // number_of), total * portions[0] // sum(portions)))
    least = 1 if total - largest >= number_of - 1 else 0
    given, rest = [largest] + [least] * (number_of - 1), total - largest - least * (number_of - 1)
    while rest > 0:
        movable = [i for i in range(1, number_of) if given[i] < largest] or [i for i in range(1, number_of) if given[i] < limit]
        pool, budget = sum([portions[i] for i in movable]), rest
        for i in movable:
            addition = min(limit - given[i], max(1, budget * portions[i] // pool), rest)
            given[i] = given[i] + addition
            rest = rest - addition
    return np.array(given)


def noise(rng, dims, deviation, reach, pieces=(), kind=jnp.bfloat16):
    values = jax.random.normal(rng, dims, jnp.float32) * deviation
    if len(pieces) > 0:
        values = block_scale(rng, dims, pieces, -0.22, 0.18) * values
    return jnp.clip(values, min=-reach, max=reach).astype(kind)


def setup_inputs(seed: int = 0) -> dict:
    seeds = jax.random.split(jax.random.key(seed), 7)
    tokens = noise(seeds[0], (TOKENS, D), 1.0, 6.0, ((0, 32),))
    expert_ids_keys = jax.random.split(jax.random.fold_in(seeds[1], 1), TOKENS // TOK_DEV)
    expert_ids_turns = jax.random.permutation(jax.random.fold_in(seeds[1], 3), TOKENS // TOK_DEV)
    expert_ids = jax.vmap(lambda own, number: shared_out(jax.random.fold_in(seeds[1], 2), own, number, TOK_DEV, EXPERTS, TOP, SRC_CAP, 2))(expert_ids_keys, expert_ids_turns).reshape((TOKENS, TOP))
    gates = jnp.clip(0.099609375 + 0.9003906 * jax.random.uniform(seeds[2], (TOKENS, TOP), jnp.float32) ** block_scale(seeds[2], (TOKENS, TOP), ((0, 32),), -0.2, 0.2), 0.099609375, 1.0).astype(jnp.bfloat16)
    w_gate = noise(seeds[3], (EXPERTS, D, FF), D ** -0.5, 0.109375, ((0, 8),))
    w_up = noise(seeds[4], (EXPERTS, D, FF), D ** -0.5, 0.109375, ((0, 8),))
    w_down = noise(seeds[5], (EXPERTS, FF, D), FF ** -0.5, 0.15625, ((0, 8),))
    return dict(tokens=tokens, expert_ids=expert_ids, gates=gates, w_gate=w_gate, w_up=w_up, w_down=w_down)


def reference(tokens, expert_ids, gates, w_gate, w_up, w_down):
    total = tokens.shape[0]
    buffer = N_DP * CAP
    onehot = expert_ids[:, :, None] == jnp.arange(EXPERTS, dtype=jnp.int32)[None, None, :]
    table = jnp.sum(gates.astype(jnp.float32)[:, :, None] * onehot.astype(jnp.float32), axis=1)
    token_index = jnp.arange(total, dtype=jnp.int32)

    def per_expert(expert, mixed_sum):
        column = lax.dynamic_index_in_dim(table, expert, 1, keepdims=False)
        routed = column > 0
        position = jnp.cumsum(routed.astype(jnp.int32)) - 1
        count = jnp.sum(routed.astype(jnp.int32))
        target = jnp.where(routed, position, buffer).astype(jnp.int32)
        slot_tok = jnp.zeros((buffer,), jnp.int32).at[target].set(token_index, mode="drop")
        slot_weight = jnp.where(jnp.arange(buffer, dtype=jnp.int32) < count, column[slot_tok], jnp.float32(0.0))
        gate_mat = lax.dynamic_index_in_dim(w_gate, expert, 0, keepdims=False)
        up_mat = lax.dynamic_index_in_dim(w_up, expert, 0, keepdims=False)
        down_mat = lax.dynamic_index_in_dim(w_down, expert, 0, keepdims=False)
        blocks = (count + BLOCK - 1) // BLOCK

        def per_block(index, acc):
            rows_idx = lax.dynamic_slice_in_dim(slot_tok, (index * BLOCK).astype(jnp.int32), BLOCK)
            weight = lax.dynamic_slice_in_dim(slot_weight, (index * BLOCK).astype(jnp.int32), BLOCK)
            rows = tokens[rows_idx]
            gate_val = jnp.dot(rows, gate_mat, preferred_element_type=jnp.float32)
            up_val = jnp.dot(rows, up_mat, preferred_element_type=jnp.float32)
            hidden = (jax.nn.silu(gate_val) * up_val).astype(jnp.bfloat16)
            result = jnp.dot(hidden, down_mat, preferred_element_type=jnp.float32)
            return acc.at[rows_idx].add(result * weight[:, None])

        return lax.fori_loop(jnp.int32(0), blocks.astype(jnp.int32), per_block, mixed_sum)

    mixed_sum = lax.fori_loop(0, EXPERTS, per_expert, jnp.zeros((total, D), jnp.float32))
    expert_load = jnp.sum(onehot.astype(jnp.int32), axis=(0, 1)).astype(jnp.int32)
    return mixed_sum.astype(jnp.bfloat16), expert_load
```

```python
import functools

import jax
import jax.numpy as jnp
from jax import lax
from jax.experimental import pallas as pl
from jax.experimental.pallas import tpu as pltpu
from jax.sharding import PartitionSpec as P

MESH = pl.DeviceIdType.MESH
LANES = 128
PIECES = 2
FF_TILE = 512
OUT_TILE = 512


def tiles(total, size):
    return [(at, min(size, total - at)) for at in range(0, total, size)]


def kernel(
    chips, n_dp, ext_hbm, wg_hbm, wu_hbm, wd_hbm, out_hbm, load_ref,
    tok, wg, wu, wd, hidden, own, sib_out, sib_in, sums_in, counts,
    tok_recv, pair_recv, send_right, send_left, send_pair, sib_send, sib_recv,
    sums_recv, sums_send, w_sem, local_sem, count_send, count_recv,
):
    rows = tok.shape[1] // 2
    width = wd.shape[1]
    ff = wd.shape[0]
    tail_at = tok.shape[2] - LANES
    gate_lane = width - tail_at
    piece = rows // PIECES
    e = lax.axis_index("expert")
    group = lax.axis_index("dp")
    pos = e // 2
    lane = e % 2
    pair = {"expert": e + 1 - 2 * lane}
    right = {"expert": e + 2}
    left = {"expert": e - 2}
    has_left = pos > 0
    has_right = pos < chips - 1
    middle = jnp.logical_and(has_left, has_right)

    weights = [
        pltpu.make_async_copy(src, dst, w_sem.at[i])
        for i, (src, dst) in enumerate(((wg_hbm, wg), (wu_hbm, wu), (wd_hbm, wd)))
    ]
    mine = pltpu.make_async_copy(ext_hbm, tok.at[pos, pl.ds(0, rows)], local_sem.at[0])
    mine.start()
    for copy in weights:
        copy.start()

    barrier = pltpu.get_barrier_semaphore()
    pl.semaphore_signal(barrier, inc=1, device_id=pair, device_id_type=MESH)
    for i in range(1, n_dp):
        peer = {"dp": (group + i) % n_dp}
        pl.semaphore_signal(barrier, inc=1, device_id=peer, device_id_type=MESH)

    @pl.when(has_left)
    def _():
        pl.semaphore_signal(barrier, inc=1, device_id=left, device_id_type=MESH)

    @pl.when(has_right)
    def _():
        pl.semaphore_signal(barrier, inc=1, device_id=right, device_id_type=MESH)

    neighbours = (pos + chips - 1) // chips + (2 * chips - 2 - pos) // chips
    pl.semaphore_wait(barrier, n_dp + neighbours)

    def tok_copy(d, target, send, to_pair=False):
        return pltpu.make_async_remote_copy(
            src_ref=tok.at[d, pl.ds(0, rows)],
            dst_ref=tok.at[d, pl.ds(rows if to_pair else 0, rows)],
            send_sem=send.at[d],
            recv_sem=(pair_recv if to_pair else tok_recv).at[d],
            device_id=target,
            device_id_type=MESH,
        )

    def sib_copy(d):
        return pltpu.make_async_remote_copy(
            src_ref=sib_out.at[d],
            dst_ref=sib_in.at[d],
            send_sem=sib_send.at[d],
            recv_sem=sib_recv.at[d],
            device_id=pair,
            device_id_type=MESH,
        )

    def sum_copy(d, q, slot, target):
        part = pl.ds(q * piece, piece)
        return pltpu.make_async_remote_copy(
            src_ref=sib_out.at[d, part],
            dst_ref=sums_in.at[slot, part],
            send_sem=sums_send.at[d, q],
            recv_sem=sums_recv.at[slot, q],
            device_id=target,
            device_id_type=MESH,
        )

    def send_sum(d, q):
        @pl.when(d > pos)
        def _():
            sum_copy(d, q, d + 1, right).start()

        @pl.when(d < pos)
        def _():
            sum_copy(d, q, d, left).start()

    def pair_sum(d, part):
        return own[d, part].astype(jnp.float32) + sib_in[d, part].astype(jnp.float32)

    def compute(d):
        x = tok.at[d]
        tail = x[:, pl.ds(tail_at, LANES)].astype(jnp.float32)
        at = lax.broadcasted_iota(jnp.int32, tail.shape, 1)
        column = jnp.sum(jnp.where(at == gate_lane + e, tail, 0.0), axis=1, keepdims=True)
        counts[group] += jnp.sum(jnp.where(tail > 0, 1.0, 0.0), axis=0, keepdims=True)
        for start, size in tiles(ff, FF_TILE):
            cols = pl.ds(start, size)
            g = jnp.dot(x[:, pl.ds(0, width)], wg[:, cols], preferred_element_type=jnp.float32)
            u = jnp.dot(x[:, pl.ds(0, width)], wu[:, cols], preferred_element_type=jnp.float32)
            hidden[:, cols] = (g / (1.0 + jnp.exp(-g)) * u).astype(jnp.bfloat16)
        for start, size in tiles(width, OUT_TILE):
            cols = pl.ds(start, size)
            y = jnp.dot(hidden[...], wd[:, cols], preferred_element_type=jnp.float32) * column
            own[d, :, cols] = y[:rows].astype(own.dtype)
            sib_out[d, :, cols] = y[rows:].astype(jnp.bfloat16)
        sib_copy(d).start()

    def arrive(d):
        tok_copy(d, pair, send_pair).wait_recv()

        @pl.when(jnp.logical_and(d < pos, has_right))
        def _():
            tok_copy(d, right, send_right).start()

        @pl.when(jnp.logical_and(d > pos, has_left))
        def _():
            tok_copy(d, left, send_left).start()

        tok_copy(d, pair, send_pair, True).start()

    counts[group] = jnp.zeros((1, LANES), jnp.float32)
    mine.wait()

    @pl.when(has_right)
    def _():
        tok_copy(pos, right, send_right).start()

    @pl.when(has_left)
    def _():
        tok_copy(pos, left, send_left).start()

    tok_copy(pos, pair, send_pair, True).start()
    for copy in weights:
        copy.wait()

    def step(t, carry):
        far = (t + 1) // 2
        d = pos + (1 - 2 * (t % 2)) * far

        @pl.when(t % 2 == 1)
        def _():
            @pl.when(pos - far >= 0)
            def _():
                arrive(pos - far)

            @pl.when(pos + far < chips)
            def _():
                arrive(pos + far)

        @pl.when(jnp.logical_and(d >= 0, d < chips))
        def _():
            tok_copy(d, pair, send_pair, True).wait_recv()
            compute(d)

            @pl.when(jnp.logical_and(t > 0, jnp.logical_not(middle)))
            def _():
                sib_copy(d).wait()
                for q in range(PIECES):
                    part = pl.ds(q * piece, piece)
                    sib_out[d, part] = pair_sum(d, part).astype(jnp.bfloat16)
                    send_sum(d, q)

        return carry

    lax.fori_loop(0, 2 * chips - 1, step, 0)

    def count_copy(i, slot):
        return pltpu.make_async_remote_copy(
            src_ref=counts.at[group],
            dst_ref=counts.at[slot],
            send_sem=count_send.at[i],
            recv_sem=count_recv.at[slot],
            device_id={"dp": (group + i) % n_dp},
            device_id_type=MESH,
        )

    for i in range(1, n_dp):
        count_copy(i, group).start()

    @pl.when(middle)
    def _():
        def forward(u, carry):
            late = (2 * pos) // chips
            past_right = (pos + 1 + u) // chips
            past_left = (u + chips - pos) // chips
            rights_first = (1 - past_right) * (pos + 1 + u) + past_right * (chips - 2 - u)
            lefts_first = (1 - past_left) * (pos - 1 - u) + past_left * (u + 1)
            d = (1 - late) * rights_first + late * lefts_first
            slot = d + (d + chips - pos) // chips
            sib_copy(d).wait()
            for q in range(PIECES):
                part = pl.ds(q * piece, piece)
                sum_copy(d, q, slot, pair).wait_recv()
                total = pair_sum(d, part) + sums_in[slot, part].astype(jnp.float32)
                sib_out[d, part] = total.astype(jnp.bfloat16)
                send_sum(d, q)
            return carry

        lax.fori_loop(0, chips - 1, forward, 0)

    sib_copy(pos).wait()
    for q in range(PIECES):
        part = pl.ds(q * piece, piece)

        def from_left(q=q, part=part):
            sum_copy(pos, q, pos + 1, pair).wait_recv()
            return sums_in[pos + 1, part].astype(jnp.float32)

        def from_right(q=q, part=part):
            sum_copy(pos, q, pos, pair).wait_recv()
            return sums_in[pos, part].astype(jnp.float32)

        @pl.when(middle)
        def _():
            total = pair_sum(pos, part) + from_left() + from_right()
            sib_out[pos, part] = total.astype(jnp.bfloat16)

        @pl.when(jnp.logical_not(has_left))
        def _():
            sib_out[pos, part] = (pair_sum(pos, part) + from_right()).astype(jnp.bfloat16)

        @pl.when(jnp.logical_not(has_right))
        def _():
            sib_out[pos, part] = (pair_sum(pos, part) + from_left()).astype(jnp.bfloat16)

    result = pltpu.make_async_copy(sib_out.at[pos], out_hbm, local_sem.at[1])
    result.start()

    load = counts[group]
    for i in range(1, n_dp):
        count_copy(i, (group + i) % n_dp).wait_recv()
        load = load + counts[(group + i) % n_dp]
    load_ref[...] = load
    for i in range(1, n_dp):
        count_copy(i, group).wait_send()

    def drain(d, carry):
        tok_copy(d, pair, send_pair, True).wait_send()

        @pl.when(jnp.logical_and(d <= pos, has_right))
        def _():
            tok_copy(d, right, send_right).wait_send()

        @pl.when(jnp.logical_and(d >= pos, has_left))
        def _():
            tok_copy(d, left, send_left).wait_send()

        for q in range(PIECES):

            @pl.when(d > pos)
            def _():
                sum_copy(d, q, d, right).wait_send()

            @pl.when(d < pos)
            def _():
                sum_copy(d, q, d, left).wait_send()

        return carry

    lax.fori_loop(0, chips, drain, 0)
    result.wait()


def shards(n_dp, n_experts, tokens, expert_ids, gates, w_gate, w_up, w_down):
    rows, width = tokens.shape
    ff = w_gate.shape[2]
    chips = n_experts // 2
    full = -(-(width + n_experts) // LANES) * LANES
    experts = jnp.arange(n_experts, dtype=jnp.int32)
    onehot = expert_ids[:, :, None] == experts[None, None, :]
    table = jnp.sum(gates.astype(jnp.float32)[:, :, None] * onehot.astype(jnp.float32), axis=1)
    blank = jnp.zeros((rows, full - width - n_experts), jnp.bfloat16)
    ext = jnp.concatenate([tokens, table.astype(jnp.bfloat16), blank], axis=1)
    bf16 = jnp.bfloat16
    dma = pltpu.SemaphoreType.DMA
    flops = 2 * chips * 2 * rows * 3 * width * ff
    mixed, load = pl.pallas_call(
        functools.partial(kernel, chips, n_dp),
        out_shape=(
            jax.ShapeDtypeStruct((rows, width), bf16),
            jax.ShapeDtypeStruct((1, LANES), jnp.float32),
        ),
        in_specs=[pl.BlockSpec(memory_space=pl.ANY)] * 4,
        out_specs=(
            pl.BlockSpec(memory_space=pl.ANY),
            pl.BlockSpec(memory_space=pltpu.VMEM),
        ),
        scratch_shapes=[
            pltpu.VMEM((chips, 2 * rows, full), bf16),
            pltpu.VMEM((width, ff), bf16),
            pltpu.VMEM((width, ff), bf16),
            pltpu.VMEM((ff, width), bf16),
            pltpu.VMEM((2 * rows, ff), bf16),
            pltpu.VMEM((chips, rows, width), jnp.float32 if chips <= 4 else bf16),
            pltpu.VMEM((chips, rows, width), bf16),
            pltpu.VMEM((chips, rows, width), bf16),
            pltpu.VMEM((chips + 1, rows, width), bf16),
            pltpu.VMEM((n_dp, 1, LANES), jnp.float32),
            dma((chips,)),
            dma((chips,)),
            dma((chips,)),
            dma((chips,)),
            dma((chips,)),
            dma((chips,)),
            dma((chips,)),
            dma((chips + 1, PIECES)),
            dma((chips, PIECES)),
            dma((3,)),
            dma((2,)),
            dma((n_dp,)),
            dma((n_dp,)),
        ],
        compiler_params=pltpu.CompilerParams(
            collective_id=0, has_side_effects=True, vmem_limit_bytes=(64 << 20) - (256 << 10)
        ),
        cost_estimate=pl.CostEstimate(
            flops=flops, bytes_accessed=6 * width * ff, transcendentals=4 * chips * rows * ff
        ),
    )(ext, w_gate[0], w_up[0], w_down[0])
    gate_lane = width - (full - LANES)
    return mixed, load[0, gate_lane : gate_lane + n_experts].astype(jnp.int32)


def solution(mesh):
    placed = (
        P(("dp", "expert"), None),
        P(("dp", "expert"), None),
        P(("dp", "expert"), None),
        P("expert", None, None),
        P("expert", None, None),
        P("expert", None, None),
    )
    return jax.shard_map(
        functools.partial(shards, mesh.shape["dp"], mesh.shape["expert"]),
        mesh=mesh,
        in_specs=placed,
        out_specs=(P(("dp", "expert"), None), P()),
        check_vma=False,
    )
```

```python
import functools

import jax
import jax.numpy as jnp
from jax import lax
from jax.experimental import pallas as pl
from jax.experimental.pallas import tpu as pltpu
from jax.sharding import PartitionSpec as P

MESH = pl.DeviceIdType.MESH
LANES = 128
PIECES = 4
FF_TILE = 512
OUT_TILE = 512


def tiles(total, size):
    return [(at, min(size, total - at)) for at in range(0, total, size)]


def dot_rows(a, b):
    return lax.dot_general(a, b, (((1,), (1,)), ((), ())), preferred_element_type=jnp.float32)


def kernel(
    chips, n_dp, ext_hbm, wg_hbm, wu_hbm, wd_hbm, out_hbm, load_ref,
    tok, wg, wu, wd, hidden, own, sib_out, sib_in, sums_in, counts,
    tok_recv, pair_recv, send_right, send_left, send_pair, sib_send, sib_recv,
    sums_recv, sums_send, w_sem, local_sem, count_send, count_recv,
):
    rows = tok.shape[1] // 2
    width = wd.shape[1]
    ff = wd.shape[0]
    tail_at = tok.shape[2] - LANES
    gate_lane = width - tail_at
    piece = rows // PIECES
    e = lax.axis_index("expert")
    group = lax.axis_index("dp")
    pos = e // 2
    lane = e % 2
    pair = {"expert": e + 1 - 2 * lane}
    right = {"expert": e + 2}
    left = {"expert": e - 2}
    has_left = pos > 0
    has_right = pos < chips - 1
    middle = jnp.logical_and(has_left, has_right)

    weights = [
        pltpu.make_async_copy(src, dst, w_sem.at[i])
        for i, (src, dst) in enumerate(((wg_hbm, wg), (wu_hbm, wu), (wd_hbm, wd)))
    ]
    mine = pltpu.make_async_copy(ext_hbm, tok.at[pos, pl.ds(0, rows)], local_sem.at[0])
    mine.start()
    for copy in weights:
        copy.start()

    barrier = pltpu.get_barrier_semaphore()
    pl.semaphore_signal(barrier, inc=1, device_id=pair, device_id_type=MESH)
    for i in range(1, n_dp):
        peer = {"dp": (group + i) % n_dp}
        pl.semaphore_signal(barrier, inc=1, device_id=peer, device_id_type=MESH)

    @pl.when(has_left)
    def _():
        pl.semaphore_signal(barrier, inc=1, device_id=left, device_id_type=MESH)

    @pl.when(has_right)
    def _():
        pl.semaphore_signal(barrier, inc=1, device_id=right, device_id_type=MESH)

    neighbours = (pos + chips - 1) // chips + (2 * chips - 2 - pos) // chips
    pl.semaphore_wait(barrier, n_dp + neighbours)

    def tok_copy(d, target, send, to_pair=False):
        return pltpu.make_async_remote_copy(
            src_ref=tok.at[d, pl.ds(0, rows)],
            dst_ref=tok.at[d, pl.ds(rows if to_pair else 0, rows)],
            send_sem=send.at[d],
            recv_sem=(pair_recv if to_pair else tok_recv).at[d],
            device_id=target,
            device_id_type=MESH,
        )

    def sib_copy(d):
        return pltpu.make_async_remote_copy(
            src_ref=sib_out.at[d],
            dst_ref=sib_in.at[d],
            send_sem=sib_send.at[d],
            recv_sem=sib_recv.at[d],
            device_id=pair,
            device_id_type=MESH,
        )

    def sum_copy(d, q, slot, target):
        part = pl.ds(q * piece, piece)
        return pltpu.make_async_remote_copy(
            src_ref=sib_out.at[d, part],
            dst_ref=sums_in.at[slot, part],
            send_sem=sums_send.at[d, q],
            recv_sem=sums_recv.at[slot, q],
            device_id=target,
            device_id_type=MESH,
        )

    def send_sum(d, q):
        @pl.when(d > pos)
        def _():
            sum_copy(d, q, d + 1, right).start()

        @pl.when(d < pos)
        def _():
            sum_copy(d, q, d, left).start()

    def pair_sum(d, part):
        return own[d, part].astype(jnp.float32) + sib_in[d, part].astype(jnp.float32)

    def compute(d):
        x = tok.at[d]
        tail = x[:, pl.ds(tail_at, LANES)].astype(jnp.float32)
        at = lax.broadcasted_iota(jnp.int32, tail.shape, 1)
        column = jnp.sum(jnp.where(at == gate_lane + e, tail, 0.0), axis=1, keepdims=True)
        counts[group] += jnp.sum(jnp.where(tail > 0, 1.0, 0.0), axis=0, keepdims=True)
        for start, size in tiles(ff, FF_TILE):
            cols = pl.ds(start, size)
            g = dot_rows(x[:, pl.ds(0, width)], wg[cols])
            u = dot_rows(x[:, pl.ds(0, width)], wu[cols])
            hidden[:, cols] = (g / (1.0 + jnp.exp(-g)) * u).astype(jnp.bfloat16)
        for start, size in tiles(width, OUT_TILE):
            cols = pl.ds(start, size)
            y = jnp.dot(hidden[...], wd[:, cols], preferred_element_type=jnp.float32) * column
            own[d, :, cols] = y[:rows].astype(own.dtype)
            sib_out[d, :, cols] = y[rows:].astype(jnp.bfloat16)
        sib_copy(d).start()

    def arrive(d):
        tok_copy(d, pair, send_pair).wait_recv()

        @pl.when(jnp.logical_and(d < pos, has_right))
        def _():
            tok_copy(d, right, send_right).start()

        @pl.when(jnp.logical_and(d > pos, has_left))
        def _():
            tok_copy(d, left, send_left).start()

        tok_copy(d, pair, send_pair, True).start()

    counts[group] = jnp.zeros((1, LANES), jnp.float32)
    mine.wait()

    @pl.when(has_right)
    def _():
        tok_copy(pos, right, send_right).start()

    @pl.when(has_left)
    def _():
        tok_copy(pos, left, send_left).start()

    tok_copy(pos, pair, send_pair, True).start()
    for copy in weights:
        copy.wait()

    def step(t, carry):
        far = ((t + 1) // 2) % chips
        d = pos + (1 - 2 * (t % 2)) * far

        @pl.when(jnp.logical_and(t % 2 == 1, t < 2 * chips - 1))
        def _():
            @pl.when(pos - far >= 0)
            def _():
                arrive(pos - far)

            @pl.when(pos + far < chips)
            def _():
                arrive(pos + far)

        @pl.when(jnp.logical_and(d >= 0, d < chips))
        def _():
            tok_copy(d, pair, send_pair, True).wait_recv()
            compute(d)

            @pl.when(jnp.logical_and(t < 2 * chips - 1, jnp.logical_not(middle)))
            def _():
                sib_copy(d).wait()
                for q in range(PIECES):
                    part = pl.ds(q * piece, piece)
                    sib_out[d, part] = pair_sum(d, part).astype(jnp.bfloat16)
                    send_sum(d, q)

        return carry

    lax.fori_loop(1, 2 * chips, step, 0)

    def count_copy(i, slot):
        return pltpu.make_async_remote_copy(
            src_ref=counts.at[group],
            dst_ref=counts.at[slot],
            send_sem=count_send.at[i],
            recv_sem=count_recv.at[slot],
            device_id={"dp": (group + i) % n_dp},
            device_id_type=MESH,
        )

    for i in range(1, n_dp):
        count_copy(i, group).start()

    @pl.when(middle)
    def _():
        def forward(u, carry):
            late = (2 * pos) // chips
            past_right = (pos + 1 + u) // chips
            past_left = (u + chips - pos) // chips
            rights_first = (1 - past_right) * (pos + 1 + u) + past_right * (chips - 2 - u)
            lefts_first = (1 - past_left) * (pos - 1 - u) + past_left * (u + 1)
            d = (1 - late) * rights_first + late * lefts_first
            slot = d + (d + chips - pos) // chips
            sib_copy(d).wait()
            for q in range(PIECES):
                part = pl.ds(q * piece, piece)
                sum_copy(d, q, slot, pair).wait_recv()
                total = pair_sum(d, part) + sums_in[slot, part].astype(jnp.float32)
                sib_out[d, part] = total.astype(jnp.bfloat16)
                send_sum(d, q)
            return carry

        lax.fori_loop(0, chips - 1, forward, 0)

    sib_copy(pos).wait()
    for q in range(PIECES):
        part = pl.ds(q * piece, piece)

        def from_left(q=q, part=part):
            sum_copy(pos, q, pos + 1, pair).wait_recv()
            return sums_in[pos + 1, part].astype(jnp.float32)

        def from_right(q=q, part=part):
            sum_copy(pos, q, pos, pair).wait_recv()
            return sums_in[pos, part].astype(jnp.float32)

        @pl.when(middle)
        def _():
            total = pair_sum(pos, part) + from_left() + from_right()
            sib_out[pos, part] = total.astype(jnp.bfloat16)

        @pl.when(jnp.logical_not(has_left))
        def _():
            sib_out[pos, part] = (pair_sum(pos, part) + from_right()).astype(jnp.bfloat16)

        @pl.when(jnp.logical_not(has_right))
        def _():
            sib_out[pos, part] = (pair_sum(pos, part) + from_left()).astype(jnp.bfloat16)

    result = pltpu.make_async_copy(sib_out.at[pos], out_hbm, local_sem.at[1])
    result.start()

    load = counts[group]
    for i in range(1, n_dp):
        count_copy(i, (group + i) % n_dp).wait_recv()
        load = load + counts[(group + i) % n_dp]
    load_ref[...] = load
    for i in range(1, n_dp):
        count_copy(i, group).wait_send()

    def drain(d, carry):
        tok_copy(d, pair, send_pair, True).wait_send()

        @pl.when(jnp.logical_and(d <= pos, has_right))
        def _():
            tok_copy(d, right, send_right).wait_send()

        @pl.when(jnp.logical_and(d >= pos, has_left))
        def _():
            tok_copy(d, left, send_left).wait_send()

        for q in range(PIECES):

            @pl.when(d > pos)
            def _():
                sum_copy(d, q, d, right).wait_send()

            @pl.when(d < pos)
            def _():
                sum_copy(d, q, d, left).wait_send()

        return carry

    lax.fori_loop(0, chips, drain, 0)
    result.wait()


def shards(n_dp, n_experts, tokens, expert_ids, gates, w_gate, w_up, w_down):
    rows, width = tokens.shape
    ff = w_gate.shape[2]
    chips = n_experts // 2
    full = -(-(width + n_experts) // LANES) * LANES
    experts = jnp.arange(n_experts, dtype=jnp.int32)
    onehot = expert_ids[:, :, None] == experts[None, None, :]
    table = jnp.sum(gates.astype(jnp.float32)[:, :, None] * onehot.astype(jnp.float32), axis=1)
    blank = jnp.zeros((rows, full - width - n_experts), jnp.bfloat16)
    ext = jnp.concatenate([tokens, table.astype(jnp.bfloat16), blank], axis=1)
    bf16 = jnp.bfloat16
    dma = pltpu.SemaphoreType.DMA
    flops = 2 * chips * 2 * rows * 3 * width * ff
    mixed, load = pl.pallas_call(
        functools.partial(kernel, chips, n_dp),
        out_shape=(
            jax.ShapeDtypeStruct((rows, width), bf16),
            jax.ShapeDtypeStruct((1, LANES), jnp.float32),
        ),
        in_specs=[pl.BlockSpec(memory_space=pl.ANY)] * 4,
        out_specs=(
            pl.BlockSpec(memory_space=pl.ANY),
            pl.BlockSpec(memory_space=pltpu.VMEM),
        ),
        scratch_shapes=[
            pltpu.VMEM((chips, 2 * rows, full), bf16),
            pltpu.VMEM((ff, width), bf16),
            pltpu.VMEM((ff, width), bf16),
            pltpu.VMEM((ff, width), bf16),
            pltpu.VMEM((2 * rows, ff), bf16),
            pltpu.VMEM((chips, rows, width), jnp.float32 if chips <= 4 else bf16),
            pltpu.VMEM((chips, rows, width), bf16),
            pltpu.VMEM((chips, rows, width), bf16),
            pltpu.VMEM((chips + 1, rows, width), bf16),
            pltpu.VMEM((n_dp, 1, LANES), jnp.float32),
            dma((chips,)),
            dma((chips,)),
            dma((chips,)),
            dma((chips,)),
            dma((chips,)),
            dma((chips,)),
            dma((chips,)),
            dma((chips + 1, PIECES)),
            dma((chips, PIECES)),
            dma((3,)),
            dma((2,)),
            dma((n_dp,)),
            dma((n_dp,)),
        ],
        compiler_params=pltpu.CompilerParams(
            collective_id=0, has_side_effects=True, vmem_limit_bytes=(64 << 20) - (256 << 10)
        ),
        cost_estimate=pl.CostEstimate(
            flops=flops, bytes_accessed=6 * width * ff, transcendentals=4 * chips * rows * ff
        ),
    )(ext, w_gate[0].T, w_up[0].T, w_down[0])
    gate_lane = width - (full - LANES)
    return mixed, load[0, gate_lane : gate_lane + n_experts].astype(jnp.int32)


def solution(mesh):
    placed = (
        P(("dp", "expert"), None),
        P(("dp", "expert"), None),
        P(("dp", "expert"), None),
        P("expert", None, None),
        P("expert", None, None),
        P("expert", None, None),
    )
    return jax.shard_map(
        functools.partial(shards, mesh.shape["dp"], mesh.shape["expert"]),
        mesh=mesh,
        in_specs=placed,
        out_specs=(P(("dp", "expert"), None), P()),
        check_vma=False,
    )
```

```python
import functools

import jax
import jax.numpy as jnp
from jax import lax
from jax.experimental import pallas as pl
from jax.experimental.pallas import tpu as pltpu
from jax.sharding import PartitionSpec as P

MESH = pl.DeviceIdType.MESH
LANES = 128
PIECES = 4
FF_TILE = 512
OUT_TILE = 512


def tiles(total, size):
    return [(at, min(size, total - at)) for at in range(0, total, size)]


def dot_rows(a, b):
    return lax.dot_general(a, b, (((1,), (1,)), ((), ())), preferred_element_type=jnp.float32)


def kernel(
    chips, n_dp, ext_hbm, wg_hbm, wu_hbm, wd_hbm, out_hbm, load_ref,
    tok, wg, wu, wd, hidden, own, sib_out, sib_in, sums_in, counts,
    tok_recv, pair_recv, send_right, send_left, send_pair, sib_send, sib_recv,
    sums_recv, sums_send, w_sem, local_sem, count_send, count_recv,
):
    rows = tok.shape[1] // 2
    width = wd.shape[1]
    ff = wd.shape[0]
    tail_at = tok.shape[2] - LANES
    gate_lane = width - tail_at
    piece = rows // PIECES
    e = lax.axis_index("expert")
    group = lax.axis_index("dp")
    pos = e // 2
    lane = e % 2
    pair = {"expert": e + 1 - 2 * lane}
    right = {"expert": e + 2}
    left = {"expert": e - 2}
    has_left = pos > 0
    has_right = pos < chips - 1
    middle = jnp.logical_and(has_left, has_right)

    weights = [
        pltpu.make_async_copy(src, dst, w_sem.at[i])
        for i, (src, dst) in enumerate(((wg_hbm, wg), (wu_hbm, wu), (wd_hbm, wd)))
    ]
    mine = pltpu.make_async_copy(ext_hbm, tok.at[pos, pl.ds(0, rows)], local_sem.at[0])
    mine.start()
    for copy in weights:
        copy.start()

    barrier = pltpu.get_barrier_semaphore()
    pl.semaphore_signal(barrier, inc=1, device_id=pair, device_id_type=MESH)
    for i in range(1, n_dp):
        peer = {"dp": (group + i) % n_dp}
        pl.semaphore_signal(barrier, inc=1, device_id=peer, device_id_type=MESH)

    @pl.when(has_left)
    def _():
        pl.semaphore_signal(barrier, inc=1, device_id=left, device_id_type=MESH)

    @pl.when(has_right)
    def _():
        pl.semaphore_signal(barrier, inc=1, device_id=right, device_id_type=MESH)

    neighbours = (pos + chips - 1) // chips + (2 * chips - 2 - pos) // chips
    pl.semaphore_wait(barrier, n_dp + neighbours)

    def tok_copy(d, target, send, to_pair=False):
        return pltpu.make_async_remote_copy(
            src_ref=tok.at[d, pl.ds(0, rows)],
            dst_ref=tok.at[d, pl.ds(rows if to_pair else 0, rows)],
            send_sem=send.at[d],
            recv_sem=(pair_recv if to_pair else tok_recv).at[d],
            device_id=target,
            device_id_type=MESH,
        )

    def sib_copy(d):
        return pltpu.make_async_remote_copy(
            src_ref=sib_out.at[d],
            dst_ref=sib_in.at[d],
            send_sem=sib_send.at[d],
            recv_sem=sib_recv.at[d],
            device_id=pair,
            device_id_type=MESH,
        )

    def sum_copy(d, q, slot, target):
        part = pl.ds(q * piece, piece)
        return pltpu.make_async_remote_copy(
            src_ref=sib_out.at[d, part],
            dst_ref=sums_in.at[slot, part],
            send_sem=sums_send.at[d, q],
            recv_sem=sums_recv.at[slot, q],
            device_id=target,
            device_id_type=MESH,
        )

    def send_sum(d, q):
        @pl.when(d > pos)
        def _():
            sum_copy(d, q, d + 1, right).start()

        @pl.when(d < pos)
        def _():
            sum_copy(d, q, d, left).start()

    def pair_sum(d, part):
        return own[d, part].astype(jnp.float32) + sib_in[d, part].astype(jnp.float32)

    def compute(d):
        x = tok.at[d]
        tail = x[:, pl.ds(tail_at, LANES)].astype(jnp.float32)
        at = lax.broadcasted_iota(jnp.int32, tail.shape, 1)
        column = jnp.sum(jnp.where(at == gate_lane + e, tail, 0.0), axis=1, keepdims=True)
        counts[group] += jnp.sum(jnp.where(tail > 0, 1.0, 0.0), axis=0, keepdims=True)
        for start, size in tiles(ff, FF_TILE):
            cols = pl.ds(start, size)
            g = dot_rows(x[:, pl.ds(0, width)], wg[cols])
            u = dot_rows(x[:, pl.ds(0, width)], wu[cols])
            hidden[:, cols] = (g / (1.0 + jnp.exp(-g)) * u).astype(jnp.bfloat16)
        for start, size in tiles(width, OUT_TILE):
            cols = pl.ds(start, size)
            y = jnp.dot(hidden[...], wd[:, cols], preferred_element_type=jnp.float32) * column
            own[d, :, cols] = y[:rows].astype(own.dtype)
            sib_out[d, :, cols] = y[rows:].astype(jnp.bfloat16)
        sib_copy(d).start()

    def arrive(d):
        tok_copy(d, pair, send_pair).wait_recv()

        @pl.when(jnp.logical_and(d < pos, has_right))
        def _():
            tok_copy(d, right, send_right).start()

        @pl.when(jnp.logical_and(d > pos, has_left))
        def _():
            tok_copy(d, left, send_left).start()

        tok_copy(d, pair, send_pair, True).start()

    def arrivals(far):
        @pl.when(pos - far >= 0)
        def _():
            arrive(pos - far)

        @pl.when(pos + far < chips)
        def _():
            arrive(pos + far)

    counts[group] = jnp.zeros((1, LANES), jnp.float32)
    mine.wait()

    @pl.when(has_right)
    def _():
        tok_copy(pos, right, send_right).start()

    @pl.when(has_left)
    def _():
        tok_copy(pos, left, send_left).start()

    tok_copy(pos, pair, send_pair, True).start()
    for copy in weights:
        copy.wait()

    def step(t, carry):
        far = ((t + 1) // 2) % chips
        d = pos + (1 - 2 * (t % 2)) * far

        @pl.when(jnp.logical_or(t == 1, jnp.logical_and(t % 2 == 0, middle)))
        def _():
            arrivals(t // 2 + 1)

        @pl.when(jnp.logical_and(d >= 0, d < chips))
        def _():
            tok_copy(d, pair, send_pair, True).wait_recv()
            compute(d)

            @pl.when(jnp.logical_and(t < 2 * chips - 1, jnp.logical_not(middle)))
            def _():
                sib_copy(d).wait()
                for q in range(PIECES):
                    part = pl.ds(q * piece, piece)
                    sib_out[d, part] = pair_sum(d, part).astype(jnp.bfloat16)
                    send_sum(d, q)

        @pl.when(jnp.logical_and(t % 2 == 0, jnp.logical_not(middle)))
        def _():
            arrivals(t // 2 + 1)

        return carry

    lax.fori_loop(1, 2 * chips, step, 0)

    def count_copy(i, slot):
        return pltpu.make_async_remote_copy(
            src_ref=counts.at[group],
            dst_ref=counts.at[slot],
            send_sem=count_send.at[i],
            recv_sem=count_recv.at[slot],
            device_id={"dp": (group + i) % n_dp},
            device_id_type=MESH,
        )

    for i in range(1, n_dp):
        count_copy(i, group).start()

    @pl.when(middle)
    def _():
        def forward(u, carry):
            late = (2 * pos) // chips
            past_right = (pos + 1 + u) // chips
            past_left = (u + chips - pos) // chips
            rights_first = (1 - past_right) * (pos + 1 + u) + past_right * (chips - 2 - u)
            lefts_first = (1 - past_left) * (pos - 1 - u) + past_left * (u + 1)
            d = (1 - late) * rights_first + late * lefts_first
            slot = d + (d + chips - pos) // chips
            sib_copy(d).wait()
            for q in range(PIECES):
                part = pl.ds(q * piece, piece)
                sum_copy(d, q, slot, pair).wait_recv()
                total = pair_sum(d, part) + sums_in[slot, part].astype(jnp.float32)
                sib_out[d, part] = total.astype(jnp.bfloat16)
                send_sum(d, q)
            return carry

        lax.fori_loop(0, chips - 1, forward, 0)

    sib_copy(pos).wait()
    for q in range(PIECES):
        part = pl.ds(q * piece, piece)

        def from_left(q=q, part=part):
            sum_copy(pos, q, pos + 1, pair).wait_recv()
            return sums_in[pos + 1, part].astype(jnp.float32)

        def from_right(q=q, part=part):
            sum_copy(pos, q, pos, pair).wait_recv()
            return sums_in[pos, part].astype(jnp.float32)

        @pl.when(middle)
        def _():
            total = pair_sum(pos, part) + from_left() + from_right()
            sib_out[pos, part] = total.astype(jnp.bfloat16)

        @pl.when(jnp.logical_not(has_left))
        def _():
            sib_out[pos, part] = (pair_sum(pos, part) + from_right()).astype(jnp.bfloat16)

        @pl.when(jnp.logical_not(has_right))
        def _():
            sib_out[pos, part] = (pair_sum(pos, part) + from_left()).astype(jnp.bfloat16)

    result = pltpu.make_async_copy(sib_out.at[pos], out_hbm, local_sem.at[1])
    result.start()

    load = counts[group]
    for i in range(1, n_dp):
        count_copy(i, (group + i) % n_dp).wait_recv()
        load = load + counts[(group + i) % n_dp]
    load_ref[...] = load
    for i in range(1, n_dp):
        count_copy(i, group).wait_send()

    def drain(d, carry):
        tok_copy(d, pair, send_pair, True).wait_send()

        @pl.when(jnp.logical_and(d <= pos, has_right))
        def _():
            tok_copy(d, right, send_right).wait_send()

        @pl.when(jnp.logical_and(d >= pos, has_left))
        def _():
            tok_copy(d, left, send_left).wait_send()

        for q in range(PIECES):

            @pl.when(d > pos)
            def _():
                sum_copy(d, q, d, right).wait_send()

            @pl.when(d < pos)
            def _():
                sum_copy(d, q, d, left).wait_send()

        return carry

    lax.fori_loop(0, chips, drain, 0)
    result.wait()


def shards(n_dp, n_experts, tokens, expert_ids, gates, w_gate, w_up, w_down):
    rows, width = tokens.shape
    ff = w_gate.shape[2]
    chips = n_experts // 2
    full = -(-(width + n_experts) // LANES) * LANES
    experts = jnp.arange(n_experts, dtype=jnp.int32)
    onehot = expert_ids[:, :, None] == experts[None, None, :]
    table = jnp.sum(gates.astype(jnp.float32)[:, :, None] * onehot.astype(jnp.float32), axis=1)
    blank = jnp.zeros((rows, full - width - n_experts), jnp.bfloat16)
    ext = jnp.concatenate([tokens, table.astype(jnp.bfloat16), blank], axis=1)
    bf16 = jnp.bfloat16
    dma = pltpu.SemaphoreType.DMA
    flops = 2 * chips * 2 * rows * 3 * width * ff
    mixed, load = pl.pallas_call(
        functools.partial(kernel, chips, n_dp),
        out_shape=(
            jax.ShapeDtypeStruct((rows, width), bf16),
            jax.ShapeDtypeStruct((1, LANES), jnp.float32),
        ),
        in_specs=[pl.BlockSpec(memory_space=pl.ANY)] * 4,
        out_specs=(
            pl.BlockSpec(memory_space=pl.ANY),
            pl.BlockSpec(memory_space=pltpu.VMEM),
        ),
        scratch_shapes=[
            pltpu.VMEM((chips, 2 * rows, full), bf16),
            pltpu.VMEM((ff, width), bf16),
            pltpu.VMEM((ff, width), bf16),
            pltpu.VMEM((ff, width), bf16),
            pltpu.VMEM((2 * rows, ff), bf16),
            pltpu.VMEM((chips, rows, width), jnp.float32 if chips <= 4 else bf16),
            pltpu.VMEM((chips, rows, width), bf16),
            pltpu.VMEM((chips, rows, width), bf16),
            pltpu.VMEM((chips + 1, rows, width), bf16),
            pltpu.VMEM((n_dp, 1, LANES), jnp.float32),
            dma((chips,)),
            dma((chips,)),
            dma((chips,)),
            dma((chips,)),
            dma((chips,)),
            dma((chips,)),
            dma((chips,)),
            dma((chips + 1, PIECES)),
            dma((chips, PIECES)),
            dma((3,)),
            dma((2,)),
            dma((n_dp,)),
            dma((n_dp,)),
        ],
        compiler_params=pltpu.CompilerParams(
            collective_id=0, has_side_effects=True, vmem_limit_bytes=(64 << 20) - (256 << 10)
        ),
        cost_estimate=pl.CostEstimate(
            flops=flops, bytes_accessed=6 * width * ff, transcendentals=4 * chips * rows * ff
        ),
    )(ext, w_gate[0].T, w_up[0].T, w_down[0])
    gate_lane = width - (full - LANES)
    return mixed, load[0, gate_lane : gate_lane + n_experts].astype(jnp.int32)


def solution(mesh):
    placed = (
        P(("dp", "expert"), None),
        P(("dp", "expert"), None),
        P(("dp", "expert"), None),
        P("expert", None, None),
        P("expert", None, None),
        P("expert", None, None),
    )
    return jax.shard_map(
        functools.partial(shards, mesh.shape["dp"], mesh.shape["expert"]),
        mesh=mesh,
        in_specs=placed,
        out_specs=(P(("dp", "expert"), None), P()),
        check_vma=False,
    )
```
